32 devices in a mesh: member: 2 (over x), region: 4 (over y, core), sub: 4 (over z).
Axes of the slice: x: 2, y: 2, z: 4, core: 2. Of those that a mesh axis runs over, the one named last changes fastest.
Arguments:
- velocity: float32 [128, 16, 2, 48, 128], P(('member', 'region'), 'sub'), parts along dimension 0, may hold values from -6 to 6
- rbf_coef: float32 [64, 16, 16, 1152], P('region', 'sub'), may hold values from -0.1875 to 0.1875
- positions: float32 [8, 4, 3, 36864], P(('member', 'region'), 'sub'), parts along dimension 0, may hold values from 0 to 16, as said below
- cell_bins: int32 [8, 4, 36864], P(('member', 'region'), 'sub'), parts along dimension 0, may hold values from 0 to 63, as said below
- live_count: int32 [8, 4], P(('member', 'region'), 'sub'), parts along dimension 0, may hold values from 2176 to 34816, as said below
- departures: int32 [8, 4, 2, 8, 128], P(('member', 'region'), 'sub'), parts along dimension 0, may hold values from -1 to 36863, as said below
Outputs:
- final_positions: float32 [8, 4, 3, 36864], P(('member', 'region'), 'sub'), parts along dimension 0
The draws below stay inside these ranges and needn't reach their ends.
There are 2 independent parts, one for each index of `member`. The reference program is written for one: setup_inputs(seed, part) draws one part's arguments, and reference() takes and returns one part's arrays. A program takes and returns all parts, laid end to end along the dimension named above; an argument that names none is the same for every part. Nothing has to cross between parts.
Inputs may be any that keep to these rules, and one draw needn't show every extreme that they name: `live_count`: one region's partitions hold exactly 34816 live particles, all others fewer; live slots are the first ones. `cell_bins`: A slot listed in departures lies in a block on the partition edge (or corner) facing its destination. `positions`: x and y lie within the slot's cell block, z between 1 and 14; a listed slot lies within 0.1 of the edge it crosses. `departures`: every listed slot is live at its substep, named once over both substeps and leaves toward a partition inside the grid; listed entries come first in each list, the rest are -1; some partition fills a list of 128 in every draw.
All inputs are finite; a program needn't handle non-finite values.
Results may differ from the reference program's by a relative error of at most 0.0003.
Values sent between devices are 32-bit elements; how exact they have to be, the bound alone decides.
A program may use at most 192 MiB of HBM per device.

```python
from functools import partial
import jax
import jax.numpy as jnp
from jax import lax

BX = 16
BY = 4
CB = 128
L = 16
NB = 16
CAP = 36864
MIG = 128
COUNT_MAX = 34816
C3L = 48
NBX = 64
NBY = 16
N_REGION = 4
N_SUB = 4


compass = ((-1, -1), (-1, 0), (-1, 1), (0, -1), (0, 1), (1, -1), (1, 0), (1, 1))


def shared_counts(key):
    busy_region = jax.random.randint(jax.random.fold_in(key, 101), (), 0, N_REGION)
    others = jax.random.randint(jax.random.fold_in(key, 102), (N_REGION, N_SUB), COUNT_MAX // 16, COUNT_MAX * 3 // 8 + 1)
    region_ids = jnp.arange(N_REGION)[:, None]
    return jnp.where(region_ids == busy_region, COUNT_MAX, others).astype(jnp.int32)


def device_list(device_key, resident, row_here, col_here):
    rank_list = jax.random.permutation(device_key, CAP)
    slot_ids = jnp.arange(CAP)
    scores = jnp.where(slot_ids < resident, rank_list, CAP + rank_list)
    ordering = jnp.argsort(scores, stable=True).astype(jnp.int32)
    per_dir = jnp.minimum(MIG, resident // 20)
    section_ids = jnp.arange(2)[:, None, None]
    dir_ids = jnp.arange(8)[None, :, None]
    slot_rank = jnp.arange(MIG)[None, None, :]
    steps_row = jnp.array([offset_pair[0] for offset_pair in compass])[None, :, None]
    steps_col = jnp.array([offset_pair[1] for offset_pair in compass])[None, :, None]
    inside = (row_here + steps_row >= 0) & (row_here + steps_row < N_REGION) & (col_here + steps_col >= 0) & (col_here + steps_col < N_SUB)
    position = (section_ids * 8 + dir_ids) * per_dir + slot_rank
    picked = ordering[jnp.minimum(position, CAP - 1)]
    usable = (slot_rank < per_dir) & inside
    return jnp.where(usable, picked, -1).astype(jnp.int32)


def shared_lists(key):
    counts = shared_counts(key)
    device_keys = jax.random.split(jax.random.fold_in(key, 301), N_REGION * N_SUB)
    row_grid = jnp.repeat(jnp.arange(N_REGION), N_SUB)
    col_grid = jnp.tile(jnp.arange(N_SUB), N_REGION)
    departure_lists = jax.vmap(device_list)(device_keys, counts.reshape(-1), row_grid, col_grid)
    return departure_lists.reshape(N_REGION, N_SUB, 2, 8, MIG)


def slot_offsets(lists_here):
    dir_ids = jnp.broadcast_to(jnp.arange(8)[None, :, None], (2, 8, MIG)).reshape(-1)
    targets = jnp.where(lists_here >= 0, lists_here, CAP).reshape(-1)
    dir_map = jnp.full((CAP + 1,), -1, jnp.int32).at[targets].set(dir_ids.astype(jnp.int32))[:CAP]
    rows_table = jnp.array([offset_pair[0] for offset_pair in compass], jnp.int32)
    cols_table = jnp.array([offset_pair[1] for offset_pair in compass], jnp.int32)
    safe_dir = jnp.maximum(dir_map, 0)
    listed = dir_map >= 0
    return (jnp.where(listed, rows_table[safe_dir], 0), jnp.where(listed, cols_table[safe_dir], 0))


def shared_bins(key):
    drawn = jax.random.randint(jax.random.fold_in(key, 201), (N_REGION, N_SUB, CAP), 0, BX * BY).astype(jnp.int32)
    lists = shared_lists(key).reshape(N_REGION * N_SUB, 2, 8, MIG)
    off_row, off_col = jax.vmap(slot_offsets)(lists)
    off_row = off_row.reshape(N_REGION, N_SUB, CAP)
    off_col = off_col.reshape(N_REGION, N_SUB, CAP)
    block_row = drawn // BY
    block_col = drawn % BY
    block_row = jnp.where(off_row < 0, 0, jnp.where(off_row > 0, BX - 1, block_row))
    block_col = jnp.where(off_col < 0, 0, jnp.where(off_col > 0, BY - 1, block_col))
    return ((block_row * BY + block_col).astype(jnp.int32), off_row, off_col)


def draw_live_count(key, part):
    counts = shared_counts(key)
    return counts


def draw_cell_bins(key, part):
    bins_drawn, off_row, off_col = shared_bins(key)
    return bins_drawn


def draw_departures(key, part):
    return shared_lists(key)


def draw_positions(key, part):
    bins_drawn, off_row, off_col = shared_bins(key)
    key = jax.random.fold_in(key, 3)
    uniform_draw = jax.random.uniform(key, (N_REGION, N_SUB, 3, CAP), jnp.float32)
    frac_x = jnp.where(off_row < 0, 0.1 * uniform_draw[:, :, 0], jnp.where(off_row > 0, 0.9 + 0.1 * uniform_draw[:, :, 0], uniform_draw[:, :, 0]))
    frac_y = jnp.where(off_col < 0, 0.1 * uniform_draw[:, :, 1], jnp.where(off_col > 0, 0.9 + 0.1 * uniform_draw[:, :, 1], uniform_draw[:, :, 1]))
    anchor_x = (bins_drawn // BY).astype(jnp.float32)
    anchor_y = (bins_drawn % BY).astype(jnp.float32)
    return jnp.stack([anchor_x + frac_x, anchor_y + frac_y, 1.0 + (L - 3) * uniform_draw[:, :, 2]], axis=2)


def shard_levels(key, extent, cuts, least, top_value):
    def one(axis_at, blocks):
        heights = jax.random.uniform(jax.random.fold_in(jax.random.fold_in(key, 6), axis_at), (blocks,), jnp.float32, least / len(cuts), top_value / len(cuts))
        return jnp.repeat(jnp.exp(heights), extent[axis_at] // blocks).reshape((-1,) + (1,) * (len(extent) - axis_at - 1))

    gain = one(*cuts[0])
    for cut in cuts[1:]:
        gain = gain * one(*cut)
    return gain


def centred(own_key, shape, scale, reach, cuts=(), kind=jnp.bfloat16):
    values = jax.random.normal(own_key, shape, jnp.float32) * scale
    if len(cuts) > 0:
        values = shard_levels(own_key, shape, cuts, -0.22, 0.18) * values
    return jnp.clip(values, min=-reach, max=reach).astype(kind)


def setup_inputs(seed: int = 0, part: int = 0) -> dict:
    key_of = jax.random.split(jax.random.key(seed), 7)
    part_keys = jax.random.split(jax.random.fold_in(key_of[6], part), 7)
    return {
        "velocity": centred(part_keys[0], (NBX, NBY, 2, C3L, CB), 1.0, 6.0, ((0, 4), (1, 4)), jnp.float32),
        "rbf_coef": centred(key_of[1], (NBX, NBY, NB, 9 * CB), (9 * CB) ** -0.5, 0.1875, ((0, 4), (1, 4)), jnp.float32),
        "positions": draw_positions(jax.random.fold_in(jax.random.fold_in(key_of[6], part), 71), part),
        "cell_bins": draw_cell_bins(jax.random.fold_in(jax.random.fold_in(key_of[6], part), 71), part),
        "live_count": draw_live_count(jax.random.fold_in(jax.random.fold_in(key_of[6], part), 71), part),
        "departures": draw_departures(jax.random.fold_in(jax.random.fold_in(key_of[6], part), 71), part),
    }


time_step = 0.1
basis_side = 4
basis_width = 0.18
compass = ((-1, -1), (-1, 0), (-1, 1), (0, -1), (0, 1), (1, -1), (1, 0), (1, 1))


def block_coefficients(padded, rbf_coef, extent_x, extent_y):
    width = padded.shape[-1]
    summed = jnp.zeros((extent_x, extent_y, 2, padded.shape[3], rbf_coef.shape[2]), jnp.float32)
    for row_shift in range(3):
        for col_shift in range(3):
            segment = 3 * row_shift + col_shift
            window = padded[row_shift:row_shift + extent_x, col_shift:col_shift + extent_y]
            weights = rbf_coef[:, :, :, segment * width:(segment + 1) * width]
            summed = summed + jnp.einsum("ijtck,ijbk->ijtcb", window, weights, precision=lax.Precision.HIGHEST)
    return summed


def evaluate(places, bins_here, coef):
    blocks = coef.shape[0]
    anchor_x = (bins_here // BY).astype(jnp.float32)
    anchor_y = (bins_here % BY).astype(jnp.float32)
    local_x = places[0] - anchor_x
    local_y = places[1] - anchor_y
    basis_ids = jnp.arange(NB)
    centre_x = ((basis_ids // basis_side).astype(jnp.float32) + 0.5) / basis_side
    centre_y = ((basis_ids % basis_side).astype(jnp.float32) + 0.5) / basis_side
    radial = jnp.exp(-((local_x[None] - centre_x[:, None]) ** 2 + (local_y[None] - centre_y[:, None]) ** 2) / basis_width)
    levels = jnp.arange(L).astype(jnp.float32)
    hat_weights = jnp.maximum(0.0, 1.0 - jnp.abs(places[2][None] - levels[:, None]))
    features = (hat_weights[:, None, :] * radial[None, :, :]).reshape(L * NB, -1)
    coef_table = coef.reshape(blocks * 3, L * NB)
    blended = jnp.dot(coef_table, features, precision=lax.Precision.HIGHEST, preferred_element_type=jnp.float32)
    blended = blended.reshape(blocks, 3, -1)
    chosen = (bins_here[None, :] == jnp.arange(blocks)[:, None]).astype(jnp.float32)
    return jnp.sum(blended * chosen[:, None, :], axis=0)


def depart_payload(values, bins, leaving, with_bins):
    usable = leaving >= 0
    safe_slots = jnp.where(usable, leaving, 0)
    picked = jnp.transpose(values[:, safe_slots], (1, 0, 2))
    row_count = values.shape[0]
    shift_list = [[float((kind % 3 == 0) * step_row * BX + (kind % 3 == 1) * step_col * BY) for kind in range(row_count)] for step_row, step_col in compass]
    shift_table = jnp.array(shift_list, dtype=jnp.float32)
    flags = usable.astype(jnp.float32)[:, None, :]
    shifted = (picked - shift_table[:, :, None]) * flags
    pieces = [shifted]
    if with_bins:
        old_bins = bins[safe_slots]
        steps_row = jnp.array([offset_pair[0] for offset_pair in compass], jnp.int32)[:, None]
        steps_col = jnp.array([offset_pair[1] for offset_pair in compass], jnp.int32)[:, None]
        block_row = jnp.clip(old_bins // BY - steps_row * BX, 0, BX - 1)
        block_col = jnp.clip(old_bins % BY - steps_col * BY, 0, BY - 1)
        carried = (block_row * BY + block_col).astype(jnp.float32)[:, None, :] * flags
        pieces.append(carried)
    pieces.append(flags)
    return jnp.concatenate(pieces, axis=1)


def land(values, bins, living, leaving, incoming, resident, base_slot, with_bins):
    row_count = values.shape[0]
    total_rows = incoming.shape[1]
    gone_slots = jnp.where(leaving >= 0, leaving, CAP).reshape(-1)
    living = living.at[gone_slots].set(0.0, mode="drop")
    arrived = jnp.transpose(incoming, (1, 0, 2)).reshape(total_rows, 8 * MIG)
    landing = (resident + base_slot).astype(jnp.int32)
    values = lax.dynamic_update_slice(values, arrived[:row_count], (jnp.int32(0), landing))
    if with_bins:
        bins = lax.dynamic_update_slice(bins, arrived[row_count].astype(jnp.int32), (landing,))
    living = lax.dynamic_update_slice(living, arrived[total_rows - 1], (landing,))
    return values, bins, living


def arrivals_whole(parcels):
    padded = jnp.pad(parcels, ((1, 1), (1, 1), (0, 0), (0, 0), (0, 0)))
    gathered = []
    for number, offset_pair in enumerate(compass):
        step_row, step_col = offset_pair
        gathered.append(padded[1 + step_row:1 + step_row + N_REGION, 1 + step_col:1 + step_col + N_SUB, 7 - number])
    return jnp.stack(gathered, axis=2)


def flatten_devices(array):
    return array.reshape((N_REGION * N_SUB,) + array.shape[2:])


def unflatten_devices(array):
    return array.reshape((N_REGION, N_SUB) + array.shape[1:])


def evaluate_all(places, bins, coef):
    result = lax.map(lambda item: evaluate(item[0], item[1], item[2]), (flatten_devices(places), flatten_devices(bins), flatten_devices(coef)))
    return unflatten_devices(result)


def migrate_all(values, bins, living, leaving, live_count, base_slot, with_bins):
    parcels = jax.vmap(jax.vmap(partial(depart_payload, with_bins=with_bins)))(values, bins, leaving)
    incoming = arrivals_whole(parcels)
    return jax.vmap(jax.vmap(partial(land, base_slot=base_slot, with_bins=with_bins)))(values, bins, living, leaving, incoming, live_count)


def reference(velocity, rbf_coef, positions, cell_bins, live_count, departures):
    padded = jnp.pad(velocity, ((1, 1), (1, 1), (0, 0), (0, 0), (0, 0)))
    coef = block_coefficients(padded, rbf_coef, NBX, NBY)
    coef = coef.reshape(N_REGION, BX, N_SUB, BY, 2, C3L, NB).transpose(0, 2, 1, 3, 4, 5, 6)
    coef = coef.reshape(N_REGION, N_SUB, BX * BY, 2, 3, L, NB)
    early = coef[:, :, :, 0]
    halfway = 0.5 * (coef[:, :, :, 0] + coef[:, :, :, 1])
    slot_ids = jnp.arange(CAP)
    living = (slot_ids[None, None, :] < live_count[:, :, None]).astype(jnp.float32)
    starts = positions * living[:, :, None, :]
    bins = cell_bins
    middle = starts + (0.5 * time_step) * evaluate_all(starts, bins, early)
    values = jnp.concatenate([starts, middle], axis=2)
    values, bins, living = migrate_all(values, bins, living, departures[:, :, 0], live_count, 0, True)
    starts = values[:, :, :3]
    middle = values[:, :, 3:]
    finals = starts + time_step * evaluate_all(middle, bins, halfway)
    finals, bins, living = migrate_all(finals, bins, living, departures[:, :, 1], live_count, 8 * MIG, False)
    return finals * living[:, :, None, :]
```

```python
import functools
import jax
import jax.numpy as jnp
from jax import lax
from jax.experimental import pallas as pl
from jax.experimental.pallas import tpu as pltpu
from jax.sharding import PartitionSpec as P

L = 16
NB = 16
MIG = 128
LANES = 128
CHUNK = 512

time_step = 0.1
compass = ((-1, -1), (-1, 0), (-1, 1), (0, -1), (0, 1), (1, -1), (1, 0), (1, 1))

MESH = pl.DeviceIdType.MESH
f32 = jnp.float32
bf16 = jnp.bfloat16
VMEM_LIMIT = 48 * 2**20


def halves(v):
    hi = v.astype(bf16)
    return hi, (v - hi.astype(f32)).astype(bf16)


def thirds(v):
    hi = v.astype(bf16)
    rest = v - hi.astype(f32)
    mid = rest.astype(bf16)
    return hi, mid, (rest - mid.astype(f32)).astype(bf16)


def mm(a, b, ca, cb):
    return lax.dot_general(a, b, (((ca,), (cb,)), ((), ())), preferred_element_type=f32)


def hot_rows(rows, which):
    ids = lax.broadcasted_iota(jnp.int32, (rows, which.shape[1]), 0)
    return jnp.where(ids == which, 1.0, 0.0)


def velocity_at(x, y, z, ax, ay, hot, table):
    width = x.shape[1]
    centre = (lax.broadcasted_iota(jnp.int32, (4, width), 0).astype(f32) + 0.5) * 0.25
    dx = (x - ax) - centre
    dy = (y - ay) - centre
    phix = jnp.exp(dx * dx * (-1.0 / 0.18))
    phiy = jnp.exp(dy * dy * (-1.0 / 0.18))
    hi, lo = halves(phix)
    hi, lo = hi.astype(f32), lo.astype(f32)
    high, low = [], []
    for j in range(4):
        high.append(hot * jnp.broadcast_to(hi[j : j + 1], hot.shape).astype(bf16))
        low.append(hot * jnp.broadcast_to(lo[j : j + 1], hot.shape).astype(bf16))
    feats = jnp.concatenate(high + high + low, axis=0)
    s = mm(table, feats, 1, 0)
    t = s[0:48] * phiy[0:1]
    for j in range(1, 4):
        t = t + s[48 * j : 48 * j + 48] * phiy[j : j + 1]
    level = lax.broadcasted_iota(jnp.int32, (L, width), 0).astype(f32)
    hat = jnp.maximum(0.0, 1.0 - jnp.abs(z - level))
    return [jnp.sum(t[16 * c : 16 * c + 16] * hat, axis=0, keepdims=True) for c in range(3)]


def anchors(n, by):
    a = n // by
    return a.astype(f32), (n - a * by).astype(f32)


def gather_kernel(pos_ref, bins_ref, list_ref, listed_ref, gone_ref, rows):
    count = pos_ref.shape[1] // LANES
    padded = rows.shape[1]
    if padded > count:
        rows[:, count:, :] = jnp.zeros((4, padded - count, LANES), f32)

    def fold(q, carry):
        at = pl.ds(pl.multiple_of(q * LANES, LANES), LANES)
        v = pos_ref[:, at]
        for k in range(3):
            rows[k, pl.ds(q, 1), :] = v[k : k + 1]
        rows[3, pl.ds(q, 1), :] = bins_ref[:, at].astype(f32)
        return carry

    lax.fori_loop(0, count, fold, 0, unroll=8)
    slots = list_ref[...]
    hi_index = slots >> 7
    lo_index = jnp.where(slots >= 0, slots & 127, -1)
    hot_hi = hot_rows(padded, hi_index).astype(bf16)
    hot_lo = hot_rows(LANES, lo_index)
    gone_ref[...] = mm(hot_hi, hot_lo.astype(bf16), 1, 1)
    for k in range(4):
        turned = rows[k].T
        parts = thirds(turned) if k < 3 else (turned.astype(bf16),)
        y = mm(parts[0], hot_hi, 1, 0)
        for part in parts[1:]:
            y = y + mm(part, hot_hi, 1, 0)
        listed_ref[k : k + 1, :] = jnp.sum(y * hot_lo, axis=0, keepdims=True)


def coef_kernel(
    vel, west, east, north, south, cwest, ceast, rbf, listed, lists, tab, pay, fin, acc, tabf
):
    bx, by = vel.shape[0], vel.shape[1]
    blocks = bx * by
    acc[...] = jnp.zeros(acc.shape, f32)

    def row(source, targets):
        for j in range(-1, by + 1):
            v = source(j)
            vhi, vlo = halves(v)
            vcat = jnp.concatenate([vhi, vlo, vhi], axis=1)
            places, pieces = [], []
            for ti, u in targets:
                safe = jnp.clip(ti, 0, bx - 1)
                for tj in range(max(0, j - 1), min(by - 1, j + 1) + 1):
                    seg = 3 * (u + 1) + (j - tj + 1)
                    pieces.append(rbf[safe, tj, :, seg * 128 : (seg + 1) * 128])
                    places.append(((ti + 1) * by + tj) * NB)
            whi, wlo = halves(jnp.concatenate(pieces, axis=0))
            out = mm(jnp.concatenate([whi, whi, wlo], axis=1), vcat, 1, 1)
            for k, place in enumerate(places):
                at = pl.ds(pl.multiple_of(place, NB), NB)
                acc[at, :] += out[k * NB : (k + 1) * NB]

    def north_at(j):
        return cwest[0, 0] if j < 0 else ceast[0, 0] if j == by else north[0, j]

    def south_at(j):
        return cwest[1, 0] if j < 0 else ceast[1, 0] if j == by else south[0, j]

    row(north_at, [(jnp.int32(0), -1)])
    row(south_at, [(jnp.int32(bx - 1), 1)])

    def inner(i, carry):
        def at(j):
            return west[i, 0] if j < 0 else east[i, 0] if j == by else vel[i, j]

        row(at, [(i - 1, 1), (i, 0), (i + 1, -1)])
        return carry

    lax.fori_loop(0, bx, inner, 0)

    for jy in range(4):
        for pair in range(2):
            both = []
            for jx in (2 * pair, 2 * pair + 1):
                both.append(acc[pl.ds(by * NB + jx * 4 + jy, blocks, stride=NB), :])
            t = jnp.concatenate(both, axis=0).T
            columns = slice(pair * 2 * blocks, (pair + 1) * 2 * blocks)
            tabf[0, jy * 48 : jy * 48 + 48, columns] = t[0:48]
            tabf[1, jy * 48 : jy * 48 + 48, columns] = 0.5 * (t[0:48] + t[48:96])
    for m in range(2):
        hi, lo = halves(tabf[m])
        tab[m] = jnp.concatenate([hi, lo, hi], axis=1)

    per = CHUNK // MIG
    for c in range(lists.shape[1] // CHUNK):
        at = slice(c * CHUNK, (c + 1) * CHUNK)
        x, y, z = listed[0:1, at], listed[1:2, at], listed[2:3, at]
        n = (listed[3:4, at] + 0.5).astype(jnp.int32)
        flags = jnp.where(lists[:, at] >= 0, 1.0, 0.0)
        ax, ay = anchors(n, by)
        hot = hot_rows(blocks, n).astype(bf16)
        u = velocity_at(x, y, z, ax, ay, hot, tab[0])
        mx, my, mz = [p + 0.5 * time_step * q for p, q in zip((x, y, z), u)]
        first = c * per
        if first < 8:
            for k in range(per):
                d = first + k
                dr, dc = compass[d]
                sl = slice(k * MIG, (k + 1) * MIG)
                fl = flags[:, sl]
                na = jnp.clip(ax[:, sl] - float(dr * bx), 0.0, float(bx - 1))
                nb = jnp.clip(ay[:, sl] - float(dc * by), 0.0, float(by - 1))
                values = [
                    x[:, sl] - float(dr * bx), y[:, sl] - float(dc * by), z[:, sl],
                    mx[:, sl] - float(dr * bx), my[:, sl] - float(dc * by), mz[:, sl],
                    na * float(by) + nb,
                ]
                for r, v in enumerate(values):
                    pay[d, r : r + 1, :] = v * fl
                pay[d, 7:8, :] = fl
        else:
            u = velocity_at(mx, my, mz, ax, ay, hot, tab[1])
            there = slice((first - 8) * MIG, (first - 8 + per) * MIG)
            for k, (p, q) in enumerate(zip((x, y, z), u)):
                fin[k : k + 1, there] = p + time_step * q


def step_kernel(
    sizes, shape, split, live, pos, bins, gone, tab, pay, fin, leaving,
    out, land0, land1, box0, box1, pay1, spread, send0, recv0, send1, recv1,
):
    regions, subs = sizes
    bx, by = shape
    blocks = bx * by
    r, s = lax.axis_index("region"), lax.axis_index("sub")

    def present(d):
        a, b = r + compass[d][0], s + compass[d][1]
        return (a >= 0) & (a < regions) & (b >= 0) & (b < subs)

    def target(d):
        return {"region": r + compass[d][0], "sub": s + compass[d][1]}

    box0[...] = jnp.zeros(box0.shape, f32)
    box1[...] = jnp.zeros(box1.shape, f32)
    barrier = pltpu.get_barrier_semaphore()
    for d in range(8):
        @pl.when(present(d))
        def _():
            pl.semaphore_signal(barrier, inc=1, device_id=target(d), device_id_type=MESH)
    peers = jnp.int32(0)
    for d in range(8):
        peers = peers + jnp.where(present(d), 1, 0)
    pl.semaphore_wait(barrier, peers)

    def parcel(d, src, box, send, recv):
        return pltpu.make_async_remote_copy(
            src_ref=src.at[d], dst_ref=box.at[7 - d], send_sem=send.at[d],
            recv_sem=recv.at[7 - d], device_id=target(d), device_id_type=MESH,
        )

    def post(src, box, send, recv):
        for d in range(8):
            @pl.when(present(d))
            def _():
                parcel(d, src, box, send, recv).start()

    def collect(src, box, send, recv):
        for d in range(8):
            @pl.when(present(d))
            def _():
                parcel(d, src, box, send, recv).wait_send()
        for d in range(8):
            @pl.when(present(d))
            def _():
                parcel(7 - d, src, box, send, recv).wait_recv()

    resident = live[0, 0]

    def bulk(i, carry):
        at = pl.ds(pl.multiple_of(i * CHUNK, CHUNK), CHUNK)
        slot = lax.broadcasted_iota(jnp.int32, (1, CHUNK), 1) + i * CHUNK
        alive = slot < resident
        v = jnp.where(alive, pos[:, at], 0.0)
        x, y, z = v[0:1], v[1:2], v[2:3]
        n = bins[:, at]
        left = jnp.concatenate(
            [gone[pl.ds(i * (CHUNK // LANES) + k, 1), :] for k in range(CHUNK // LANES)], axis=1
        )
        ax, ay = anchors(n, by)
        hot = hot_rows(blocks, n).astype(bf16)
        u = velocity_at(x, y, z, ax, ay, hot, tab[0])
        mx, my, mz = [p + 0.5 * time_step * q for p, q in zip((x, y, z), u)]
        u = velocity_at(mx, my, mz, ax, ay, hot, tab[1])
        keep = alive & (left == 0.0)
        for k, (p, q) in enumerate(zip((x, y, z), u)):
            out[k : k + 1, at] = jnp.where(keep, p + time_step * q, 0.0)
        return carry

    post(pay, box0, send0, recv0)
    lax.fori_loop(0, split, bulk, 0)
    collect(pay, box0, send0, recv0)

    per = CHUNK // MIG
    living = []
    for c in range(8 // per):
        rows = [
            jnp.concatenate([box0[c * per + k, q : q + 1, :] for k in range(per)], axis=1)
            for q in range(8)
        ]
        n = (rows[6] + 0.5).astype(jnp.int32)
        ax, ay = anchors(n, by)
        hot = hot_rows(blocks, n).astype(bf16)
        u = velocity_at(rows[3], rows[4], rows[5], ax, ay, hot, tab[1])
        living.append(rows[7])
        for k in range(3):
            f = rows[k] + time_step * u[k]
            land0[k : k + 1, c * CHUNK : (c + 1) * CHUNK] = f
            for e in range(per):
                spread[c * per + e : c * per + e + 1, k * LANES : (k + 1) * LANES] = f[
                    :, e * LANES : (e + 1) * LANES
                ]

    slots = leaving[...]
    flags = jnp.where(slots >= 0, 1.0, 0.0)
    late = slots >= resident
    rel = jnp.where(late & (slots >= 0), slots - resident, -1)
    hot_hi = hot_rows(8, rel >> 7)
    hot_lo = hot_rows(LANES, jnp.where(rel >= 0, rel & 127, -1))
    hot_bf = jnp.concatenate([hot_hi, jnp.zeros(hot_hi.shape, f32)], axis=0).astype(bf16)
    left = mm(hot_bf, hot_lo.astype(bf16), 1, 1)
    wide = spread[...]
    wide = jnp.concatenate([wide, jnp.zeros(wide.shape, f32)], axis=0)
    picked = None
    for part in thirds(wide):
        y = mm(part, hot_bf, 0, 0)
        picked = y if picked is None else picked + y
    for k in range(3):
        mine = jnp.sum(picked[k * LANES : (k + 1) * LANES] * hot_lo, axis=0, keepdims=True)
        value = jnp.where(late, mine, fin[k : k + 1, :])
        for d in range(8):
            sl = slice(d * MIG, (d + 1) * MIG)
            shift = float((bx * compass[d][0], by * compass[d][1], 0)[k])
            pay1[d, k : k + 1, :] = (value[:, sl] - shift) * flags[:, sl]
    for d in range(8):
        pay1[d, 3:4, :] = flags[:, d * MIG : (d + 1) * MIG]
        pay1[d, 4:8, :] = jnp.zeros((4, MIG), f32)

    post(pay1, box1, send1, recv1)
    for d in range(8):
        sl = slice(d * MIG, (d + 1) * MIG)
        stays = jnp.where(left[d : d + 1] == 0.0, 1.0, 0.0)
        stays = stays * living[d // per][:, (d % per) * MIG : (d % per + 1) * MIG]
        land0[:, sl] = land0[:, sl] * stays
    lax.fori_loop(split, pos.shape[1] // CHUNK, bulk, 0)
    collect(pay1, box1, send1, recv1)
    for d in range(8):
        for k in range(3):
            land1[k : k + 1, d * MIG : (d + 1) * MIG] = box1[d, k : k + 1, :] * box1[d, 3:4, :]


def body(sizes, velocity, rbf_coef, positions, cell_bins, live_count, departures):
    bx, by, _, c3l, cb = velocity.shape
    cap = positions.shape[-1]
    count = 8 * MIG
    vel = velocity.reshape(bx, by, 2 * c3l, cb)
    rbf = rbf_coef
    pos = positions[0, 0]
    bins = cell_bins.reshape(1, cap)
    lists = departures.reshape(1, 2 * count)
    vmem = pl.BlockSpec(memory_space=pltpu.VMEM)
    smem = pl.BlockSpec(memory_space=pltpu.SMEM)
    local = pltpu.CompilerParams(vmem_limit_bytes=VMEM_LIMIT)

    def shift(block, axis, up):
        size = lax.axis_size(axis)
        pairs = [(i, i + 1) for i in range(size - 1)]
        return lax.ppermute(block, axis, pairs if up else [(b, a) for a, b in pairs])

    west = shift(vel[:, by - 1 :], "sub", True)
    east = shift(vel[:, :1], "sub", False)
    north = shift(vel[bx - 1 :], "region", True)
    south = shift(vel[:1], "region", False)
    cwest = shift(jnp.concatenate([north[:, by - 1 :], south[:, by - 1 :]], axis=0), "sub", True)
    ceast = shift(jnp.concatenate([north[:, :1], south[:, :1]], axis=0), "sub", False)

    rows = -(-(cap // LANES) // 128) * 128
    listed, gone = pl.pallas_call(
        gather_kernel,
        out_shape=(
            jax.ShapeDtypeStruct((4, 2 * count), f32),
            jax.ShapeDtypeStruct((rows, LANES), f32),
        ),
        in_specs=[vmem] * 3,
        out_specs=(vmem, vmem),
        scratch_shapes=[pltpu.VMEM((4, rows, LANES), f32)],
        compiler_params=local,
        cost_estimate=pl.CostEstimate(flops=4 * 10**9, bytes_accessed=10**6, transcendentals=0),
        name="gather_lists",
    )(pos, bins, lists)

    blocks = bx * by
    tab, pay, fin = pl.pallas_call(
        coef_kernel,
        out_shape=(
            jax.ShapeDtypeStruct((2, 192, 12 * blocks), bf16),
            jax.ShapeDtypeStruct((8, 8, MIG), f32),
            jax.ShapeDtypeStruct((3, count), f32),
        ),
        in_specs=[vmem] * 10,
        out_specs=(vmem,) * 3,
        scratch_shapes=[
            pltpu.VMEM(((bx + 2) * by * NB, 2 * c3l), f32),
            pltpu.VMEM((2, 192, 4 * blocks), f32),
        ],
        compiler_params=local,
        name="coefficients",
    )(vel, west, east, north, south, cwest, ceast, rbf, listed, lists)

    out, land0, land1 = pl.pallas_call(
        functools.partial(step_kernel, sizes, (bx, by), 20),
        out_shape=(
            jax.ShapeDtypeStruct((3, cap), f32),
            jax.ShapeDtypeStruct((3, count), f32),
            jax.ShapeDtypeStruct((3, count), f32),
        ),
        in_specs=[smem] + [vmem] * 7,
        out_specs=(vmem,) * 3,
        scratch_shapes=[
            pltpu.VMEM((8, 8, MIG), f32),
            pltpu.VMEM((8, 8, MIG), f32),
            pltpu.VMEM((8, 8, MIG), f32),
            pltpu.VMEM((8, 3 * LANES), f32),
            pltpu.SemaphoreType.DMA((8,)),
            pltpu.SemaphoreType.DMA((8,)),
            pltpu.SemaphoreType.DMA((8,)),
            pltpu.SemaphoreType.DMA((8,)),
        ],
        compiler_params=pltpu.CompilerParams(
            collective_id=0, has_side_effects=True, vmem_limit_bytes=VMEM_LIMIT
        ),
        name="advect",
    )(live_count, pos, bins, gone, tab, pay, fin, lists[:, count:])
    resident = live_count[0, 0]
    out = lax.dynamic_update_slice(out, land0, (jnp.int32(0), resident))
    out = lax.dynamic_update_slice(out, land1, (jnp.int32(0), resident + count))
    return out[None, None]


def solution(mesh):
    in_specs = (
        P(("member", "region"), "sub", None, None, None),
        P("region", "sub", None, None),
        P(("member", "region"), "sub", None, None),
        P(("member", "region"), "sub", None),
        P(("member", "region"), "sub"),
        P(("member", "region"), "sub", None, None, None),
    )
    out_specs = P(("member", "region"), "sub", None, None)
    sizes = (mesh.shape["region"], mesh.shape["sub"])
    return jax.shard_map(
        functools.partial(body, sizes), mesh=mesh, in_specs=in_specs, out_specs=out_specs,
        check_vma=False,
    )
```

```python
import functools
import jax
import jax.numpy as jnp
from jax import lax
from jax.experimental import pallas as pl
from jax.experimental.pallas import tpu as pltpu
from jax.sharding import PartitionSpec as P

L = 16
NB = 16
MIG = 128
LANES = 128
CHUNK = 1024
BULK = 4096

time_step = 0.1
compass = ((-1, -1), (-1, 0), (-1, 1), (0, -1), (0, 1), (1, -1), (1, 0), (1, 1))

MESH = pl.DeviceIdType.MESH
f32 = jnp.float32
bf16 = jnp.bfloat16
VMEM_LIMIT = 48 * 2**20


def halves(v):
    hi = v.astype(bf16)
    return hi, (v - hi.astype(f32)).astype(bf16)


def thirds(v):
    hi = v.astype(bf16)
    rest = v - hi.astype(f32)
    mid = rest.astype(bf16)
    return hi, mid, (rest - mid.astype(f32)).astype(bf16)


def mm(a, b, ca, cb):
    return lax.dot_general(a, b, (((ca,), (cb,)), ((), ())), preferred_element_type=f32)


def hot_rows(rows, which):
    ids = lax.broadcasted_iota(jnp.int32, (rows, which.shape[1]), 0)
    return jnp.where(ids == which, 1.0, 0.0)


def velocity_at(x, y, z, ax, ay, hot, table):
    width = x.shape[1]
    centre = (lax.broadcasted_iota(jnp.int32, (4, width), 0).astype(f32) + 0.5) * 0.25
    dx = (x - ax) - centre
    dy = (y - ay) - centre
    phix = jnp.exp(dx * dx * (-1.0 / 0.18))
    phiy = jnp.exp(dy * dy * (-1.0 / 0.18))
    hi, lo = halves(phix)
    hi, lo = hi.astype(f32), lo.astype(f32)
    high, low = [], []
    for j in range(4):
        high.append(hot * jnp.broadcast_to(hi[j : j + 1], hot.shape).astype(bf16))
        low.append(hot * jnp.broadcast_to(lo[j : j + 1], hot.shape).astype(bf16))
    feats = jnp.concatenate(high + high + low, axis=0)
    s = mm(table, feats, 1, 0)
    t = s[0:48] * phiy[0:1]
    for j in range(1, 4):
        t = t + s[48 * j : 48 * j + 48] * phiy[j : j + 1]
    level = lax.broadcasted_iota(jnp.int32, (L, width), 0).astype(f32)
    hat = jnp.maximum(0.0, 1.0 - jnp.abs(z - level))
    return [jnp.sum(t[16 * c : 16 * c + 16] * hat, axis=0, keepdims=True) for c in range(3)]


def anchors(n, by):
    a = n // by
    return a.astype(f32), (n - a * by).astype(f32)


def gather_lists(pos_ref, bins_ref, list_ref, listed_ref, gone_ref, rows):
    count = pos_ref.shape[1] // LANES
    padded = rows.shape[1]
    if padded > count:
        rows[:, count:, :] = jnp.zeros((4, padded - count, LANES), f32)

    def fold(q, carry):
        at = pl.ds(pl.multiple_of(q * LANES, LANES), LANES)
        v = pos_ref[:, at]
        for k in range(3):
            rows[k, pl.ds(q, 1), :] = v[k : k + 1]
        rows[3, pl.ds(q, 1), :] = bins_ref[:, at].astype(f32)
        return carry

    lax.fori_loop(0, count, fold, 0, unroll=8)
    slots = list_ref[...]
    hi_index = slots >> 7
    lo_index = jnp.where(slots >= 0, slots & 127, -1)
    hot_hi = hot_rows(padded, hi_index).astype(bf16)
    hot_lo = hot_rows(LANES, lo_index)
    gone_ref[...] = mm(hot_hi, hot_lo.astype(bf16), 1, 1)
    for k in range(4):
        turned = rows[k].T
        parts = thirds(turned) if k < 3 else (turned.astype(bf16),)
        y = mm(parts[0], hot_hi, 1, 0)
        for part in parts[1:]:
            y = y + mm(part, hot_hi, 1, 0)
        listed_ref[k : k + 1, :] = jnp.sum(y * hot_lo, axis=0, keepdims=True)


def grid_peers(sizes):
    regions, subs = sizes
    r, s = lax.axis_index("region"), lax.axis_index("sub")

    def present(d):
        a, b = r + compass[d][0], s + compass[d][1]
        return (a >= 0) & (a < regions) & (b >= 0) & (b < subs)

    def target(d):
        return {"region": r + compass[d][0], "sub": s + compass[d][1]}

    return present, target


def greet(present, target):
    barrier = pltpu.get_barrier_semaphore()
    peers = jnp.int32(0)
    for d in range(8):
        peers = peers + jnp.where(present(d), 1, 0)

        @pl.when(present(d))
        def _():
            pl.semaphore_signal(barrier, inc=1, device_id=target(d), device_id_type=MESH)
    pl.semaphore_wait(barrier, peers)


def coef_kernel(
    sizes, vel, rbf, pos, bins, lists, tab, pay, fin, gone,
    west, east, north, south, corners, acc, tabf, listed, folded, send, recv,
):
    bx, by = vel.shape[0], vel.shape[1]
    blocks = bx * by
    present, target = grid_peers(sizes)
    for box in (west, east, north, south, corners):
        box[...] = jnp.zeros(box.shape, f32)
    greet(present, target)
    boxes = [corners.at[0], north, corners.at[1], west, east, corners.at[2], south, corners.at[3]]

    def halo(e):
        dr, dc = compass[e]
        row_at = 0 if dr < 0 else bx - 1
        col_at = 0 if dc < 0 else by - 1
        if dr == 0:
            src = vel.at[:, col_at]
        elif dc == 0:
            src = vel.at[row_at]
        else:
            src = vel.at[row_at, col_at]
        return pltpu.make_async_remote_copy(
            src_ref=src, dst_ref=boxes[7 - e], send_sem=send.at[e], recv_sem=recv.at[7 - e],
            device_id=target(e), device_id_type=MESH,
        )

    for e in (3, 4, 0, 2, 5, 7, 1, 6):
        @pl.when(present(e))
        def _():
            halo(e).start()

    gather_lists(pos, bins, lists, listed, gone, folded)
    acc[...] = jnp.zeros(acc.shape, f32)

    def row(source, targets, columns):
        for j in columns:
            v = source(j)
            vhi, vlo = halves(v)
            vcat = jnp.concatenate([vhi, vlo, vhi], axis=1)
            places, pieces = [], []
            for ti, u in targets:
                safe = jnp.clip(ti, 0, bx - 1)
                for tj in range(max(0, j - 1), min(by - 1, j + 1) + 1):
                    seg = 3 * (u + 1) + (j - tj + 1)
                    pieces.append(rbf[safe, tj, :, seg * 128 : (seg + 1) * 128])
                    places.append(((ti + 1) * by + tj) * NB)
            whi, wlo = halves(jnp.concatenate(pieces, axis=0))
            out = mm(jnp.concatenate([whi, whi, wlo], axis=1), vcat, 1, 1)
            for k, place in enumerate(places):
                at = pl.ds(pl.multiple_of(place, NB), NB)
                acc[at, :] += out[k * NB : (k + 1) * NB]

    def north_at(j):
        return corners[0] if j < 0 else corners[1] if j == by else north[j]

    def south_at(j):
        return corners[2] if j < 0 else corners[3] if j == by else south[j]

    def around(i):
        return [(i - 1, 1), (i, 0), (i + 1, -1)]

    def inner(i, carry):
        row(lambda j: vel[i, j], around(i), range(by))
        return carry

    def outer(i, carry):
        row(lambda j: west[i] if j < 0 else east[i], around(i), (-1, by))
        return carry

    lax.fori_loop(0, bx, inner, 0)
    for e in range(8):
        @pl.when(present(e))
        def _():
            halo(e).wait_send()
    for e in range(8):
        @pl.when(present(e))
        def _():
            halo(7 - e).wait_recv()
    row(north_at, [(jnp.int32(0), -1)], range(-1, by + 1))
    row(south_at, [(jnp.int32(bx - 1), 1)], range(-1, by + 1))
    lax.fori_loop(0, bx, outer, 0)

    for jy in range(4):
        for pair in range(2):
            both = []
            for jx in (2 * pair, 2 * pair + 1):
                both.append(acc[pl.ds(by * NB + jx * 4 + jy, blocks, stride=NB), :])
            t = jnp.concatenate(both, axis=0).T
            columns = slice(pair * 2 * blocks, (pair + 1) * 2 * blocks)
            tabf[0, jy * 48 : jy * 48 + 48, columns] = t[0:48]
            tabf[1, jy * 48 : jy * 48 + 48, columns] = 0.5 * (t[0:48] + t[48:96])
    for m in range(2):
        hi, lo = halves(tabf[m])
        tab[m] = jnp.concatenate([hi, lo, hi], axis=1)

    per = CHUNK // MIG
    for c in range(lists.shape[1] // CHUNK):
        at = slice(c * CHUNK, (c + 1) * CHUNK)
        x, y, z = listed[0:1, at], listed[1:2, at], listed[2:3, at]
        n = (listed[3:4, at] + 0.5).astype(jnp.int32)
        flags = jnp.where(lists[:, at] >= 0, 1.0, 0.0)
        ax, ay = anchors(n, by)
        hot = hot_rows(blocks, n).astype(bf16)
        u = velocity_at(x, y, z, ax, ay, hot, tab[0])
        mx, my, mz = [p + 0.5 * time_step * q for p, q in zip((x, y, z), u)]
        first = c * per
        if first < 8:
            for k in range(per):
                d = first + k
                dr, dc = compass[d]
                sl = slice(k * MIG, (k + 1) * MIG)
                fl = flags[:, sl]
                na = jnp.clip(ax[:, sl] - float(dr * bx), 0.0, float(bx - 1))
                nb = jnp.clip(ay[:, sl] - float(dc * by), 0.0, float(by - 1))
                values = [
                    x[:, sl] - float(dr * bx), y[:, sl] - float(dc * by), z[:, sl],
                    mx[:, sl] - float(dr * bx), my[:, sl] - float(dc * by), mz[:, sl],
                    na * float(by) + nb,
                ]
                for r, v in enumerate(values):
                    pay[d, r : r + 1, :] = v * fl
                pay[d, 7:8, :] = fl
        else:
            u = velocity_at(mx, my, mz, ax, ay, hot, tab[1])
            there = slice((first - 8) * MIG, (first - 8 + per) * MIG)
            for k, (p, q) in enumerate(zip((x, y, z), u)):
                fin[k : k + 1, there] = p + time_step * q


def step_kernel(
    sizes, shape, split, live, pos, bins, gone, tab, pay, fin, leaving,
    out, land0, land1, box0, box1, pay1, spread, send0, recv0, send1, recv1,
):
    bx, by = shape
    blocks = bx * by
    present, target = grid_peers(sizes)
    box0[...] = jnp.zeros(box0.shape, f32)
    box1[...] = jnp.zeros(box1.shape, f32)
    greet(present, target)

    def parcel(d, src, box, send, recv):
        return pltpu.make_async_remote_copy(
            src_ref=src.at[d], dst_ref=box.at[7 - d], send_sem=send.at[d],
            recv_sem=recv.at[7 - d], device_id=target(d), device_id_type=MESH,
        )

    def post(src, box, send, recv):
        for d in range(8):
            @pl.when(present(d))
            def _():
                parcel(d, src, box, send, recv).start()

    def collect(src, box, send, recv):
        for d in range(8):
            @pl.when(present(d))
            def _():
                parcel(d, src, box, send, recv).wait_send()
        for d in range(8):
            @pl.when(present(d))
            def _():
                parcel(7 - d, src, box, send, recv).wait_recv()

    resident = live[0, 0]

    def bulk(i, carry):
        at = pl.ds(pl.multiple_of(i * BULK, BULK), BULK)
        slot = lax.broadcasted_iota(jnp.int32, (1, BULK), 1) + i * BULK
        alive = slot < resident
        v = jnp.where(alive, pos[:, at], 0.0)
        x, y, z = v[0:1], v[1:2], v[2:3]
        n = bins[:, at]
        left = jnp.concatenate(
            [gone[pl.ds(i * (BULK // LANES) + k, 1), :] for k in range(BULK // LANES)], axis=1
        )
        ax, ay = anchors(n, by)
        hot = hot_rows(blocks, n).astype(bf16)
        u = velocity_at(x, y, z, ax, ay, hot, tab[0])
        mx, my, mz = [p + 0.5 * time_step * q for p, q in zip((x, y, z), u)]
        u = velocity_at(mx, my, mz, ax, ay, hot, tab[1])
        keep = alive & (left == 0.0)
        for k, (p, q) in enumerate(zip((x, y, z), u)):
            out[k : k + 1, at] = jnp.where(keep, p + time_step * q, 0.0)
        return carry

    post(pay, box0, send0, recv0)
    lax.fori_loop(0, split, bulk, 0)
    collect(pay, box0, send0, recv0)

    per = CHUNK // MIG
    living = []
    for c in range(8 // per):
        rows = [
            jnp.concatenate([box0[c * per + k, q : q + 1, :] for k in range(per)], axis=1)
            for q in range(8)
        ]
        n = (rows[6] + 0.5).astype(jnp.int32)
        ax, ay = anchors(n, by)
        hot = hot_rows(blocks, n).astype(bf16)
        u = velocity_at(rows[3], rows[4], rows[5], ax, ay, hot, tab[1])
        living.append(rows[7])
        for k in range(3):
            f = rows[k] + time_step * u[k]
            land0[k : k + 1, c * CHUNK : (c + 1) * CHUNK] = f
            for e in range(per):
                spread[c * per + e : c * per + e + 1, k * LANES : (k + 1) * LANES] = f[
                    :, e * LANES : (e + 1) * LANES
                ]

    slots = leaving[...]
    flags = jnp.where(slots >= 0, 1.0, 0.0)
    late = slots >= resident
    rel = jnp.where(late & (slots >= 0), slots - resident, -1)
    hot_hi = hot_rows(8, rel >> 7)
    hot_lo = hot_rows(LANES, jnp.where(rel >= 0, rel & 127, -1))
    hot_bf = jnp.concatenate([hot_hi, jnp.zeros(hot_hi.shape, f32)], axis=0).astype(bf16)
    left = mm(hot_bf, hot_lo.astype(bf16), 1, 1)
    wide = spread[...]
    wide = jnp.concatenate([wide, jnp.zeros(wide.shape, f32)], axis=0)
    picked = None
    for part in thirds(wide):
        y = mm(part, hot_bf, 0, 0)
        picked = y if picked is None else picked + y
    for k in range(3):
        mine = jnp.sum(picked[k * LANES : (k + 1) * LANES] * hot_lo, axis=0, keepdims=True)
        value = jnp.where(late, mine, fin[k : k + 1, :])
        for d in range(8):
            sl = slice(d * MIG, (d + 1) * MIG)
            shift = float((bx * compass[d][0], by * compass[d][1], 0)[k])
            pay1[d, k : k + 1, :] = (value[:, sl] - shift) * flags[:, sl]
    for d in range(8):
        pay1[d, 3:4, :] = flags[:, d * MIG : (d + 1) * MIG]
        pay1[d, 4:8, :] = jnp.zeros((4, MIG), f32)

    post(pay1, box1, send1, recv1)
    for d in range(8):
        sl = slice(d * MIG, (d + 1) * MIG)
        stays = jnp.where(left[d : d + 1] == 0.0, 1.0, 0.0)
        stays = stays * living[d // per][:, (d % per) * MIG : (d % per + 1) * MIG]
        land0[:, sl] = land0[:, sl] * stays
    lax.fori_loop(split, pos.shape[1] // BULK, bulk, 0)
    collect(pay1, box1, send1, recv1)
    for d in range(8):
        for k in range(3):
            land1[k : k + 1, d * MIG : (d + 1) * MIG] = box1[d, k : k + 1, :] * box1[d, 3:4, :]


def body(sizes, velocity, rbf_coef, positions, cell_bins, live_count, departures):
    bx, by, _, c3l, cb = velocity.shape
    cap = positions.shape[-1]
    count = 8 * MIG
    vel = velocity.reshape(bx, by, 2 * c3l, cb)
    rbf = rbf_coef
    pos = positions[0, 0]
    bins = cell_bins.reshape(1, cap)
    lists = departures.reshape(1, 2 * count)
    vmem = pl.BlockSpec(memory_space=pltpu.VMEM)
    smem = pl.BlockSpec(memory_space=pltpu.SMEM)
    rows = -(-(cap // LANES) // 128) * 128
    blocks = bx * by
    tab, pay, fin, gone = pl.pallas_call(
        functools.partial(coef_kernel, sizes),
        out_shape=(
            jax.ShapeDtypeStruct((2, 192, 12 * blocks), bf16),
            jax.ShapeDtypeStruct((8, 8, MIG), f32),
            jax.ShapeDtypeStruct((3, count), f32),
            jax.ShapeDtypeStruct((rows, LANES), f32),
        ),
        in_specs=[vmem] * 5,
        out_specs=(vmem,) * 4,
        scratch_shapes=[
            pltpu.VMEM((bx, 2 * c3l, cb), f32),
            pltpu.VMEM((bx, 2 * c3l, cb), f32),
            pltpu.VMEM((by, 2 * c3l, cb), f32),
            pltpu.VMEM((by, 2 * c3l, cb), f32),
            pltpu.VMEM((4, 2 * c3l, cb), f32),
            pltpu.VMEM(((bx + 2) * by * NB, 2 * c3l), f32),
            pltpu.VMEM((2, 192, 4 * blocks), f32),
            pltpu.VMEM((4, 2 * count), f32),
            pltpu.VMEM((4, rows, LANES), f32),
            pltpu.SemaphoreType.DMA((8,)),
            pltpu.SemaphoreType.DMA((8,)),
        ],
        compiler_params=pltpu.CompilerParams(
            collective_id=1, has_side_effects=True, vmem_limit_bytes=VMEM_LIMIT
        ),
        name="coefficients",
    )(vel, rbf, pos, bins, lists)

    out, land0, land1 = pl.pallas_call(
        functools.partial(step_kernel, sizes, (bx, by), 2),
        out_shape=(
            jax.ShapeDtypeStruct((3, cap), f32),
            jax.ShapeDtypeStruct((3, count), f32),
            jax.ShapeDtypeStruct((3, count), f32),
        ),
        in_specs=[smem] + [vmem] * 7,
        out_specs=(vmem,) * 3,
        scratch_shapes=[
            pltpu.VMEM((8, 8, MIG), f32),
            pltpu.VMEM((8, 8, MIG), f32),
            pltpu.VMEM((8, 8, MIG), f32),
            pltpu.VMEM((8, 3 * LANES), f32),
            pltpu.SemaphoreType.DMA((8,)),
            pltpu.SemaphoreType.DMA((8,)),
            pltpu.SemaphoreType.DMA((8,)),
            pltpu.SemaphoreType.DMA((8,)),
        ],
        compiler_params=pltpu.CompilerParams(
            collective_id=0, has_side_effects=True, vmem_limit_bytes=VMEM_LIMIT
        ),
        name="advect",
    )(live_count, pos, bins, gone, tab, pay, fin, lists[:, count:])
    resident = live_count[0, 0]
    out = lax.dynamic_update_slice(out, land0, (jnp.int32(0), resident))
    out = lax.dynamic_update_slice(out, land1, (jnp.int32(0), resident + count))
    return out[None, None]


def solution(mesh):
    in_specs = (
        P(("member", "region"), "sub", None, None, None),
        P("region", "sub", None, None),
        P(("member", "region"), "sub", None, None),
        P(("member", "region"), "sub", None),
        P(("member", "region"), "sub"),
        P(("member", "region"), "sub", None, None, None),
    )
    out_specs = P(("member", "region"), "sub", None, None)
    sizes = (mesh.shape["region"], mesh.shape["sub"])
    return jax.shard_map(
        functools.partial(body, sizes), mesh=mesh, in_specs=in_specs, out_specs=out_specs,
        check_vma=False,
    )
```

```python
import functools
import jax
import jax.numpy as jnp
from jax import lax
from jax.experimental import pallas as pl
from jax.experimental.pallas import tpu as pltpu
from jax.sharding import PartitionSpec as P

L = 16
NB = 16
MIG = 128
LANES = 128
CHUNK = 1024
PARTS = 8

time_step = 0.1
compass = ((-1, -1), (-1, 0), (-1, 1), (0, -1), (0, 1), (1, -1), (1, 0), (1, 1))

MESH = pl.DeviceIdType.MESH
f32 = jnp.float32
bf16 = jnp.bfloat16
VMEM_LIMIT = 56 * 2**20


def halves(v):
    hi = v.astype(bf16)
    return hi, (v - hi.astype(f32)).astype(bf16)


def thirds(v):
    hi = v.astype(bf16)
    rest = v - hi.astype(f32)
    mid = rest.astype(bf16)
    return hi, mid, (rest - mid.astype(f32)).astype(bf16)


def mm(a, b, ca, cb):
    return lax.dot_general(a, b, (((ca,), (cb,)), ((), ())), preferred_element_type=f32)


def hot_rows(rows, which):
    ids = lax.broadcasted_iota(jnp.int32, (rows, which.shape[1]), 0)
    return jnp.where(ids == which, 1.0, 0.0)


def velocity_at(x, y, z, ax, ay, hot, table):
    width = x.shape[1]
    centre = (lax.broadcasted_iota(jnp.int32, (4, width), 0).astype(f32) + 0.5) * 0.25
    dx = (x - ax) - centre
    dy = (y - ay) - centre
    phix = jnp.exp(dx * dx * (-1.0 / 0.18))
    phiy = jnp.exp(dy * dy * (-1.0 / 0.18))
    hi, lo = halves(phix)
    hi, lo = hi.astype(f32), lo.astype(f32)
    high, low = [], []
    for j in range(4):
        high.append(hot * jnp.broadcast_to(hi[j : j + 1], hot.shape).astype(bf16))
        low.append(hot * jnp.broadcast_to(lo[j : j + 1], hot.shape).astype(bf16))
    feats = jnp.concatenate(high + high + low, axis=0)
    s = mm(table, feats, 1, 0)
    t = s[0:48] * phiy[0:1]
    for j in range(1, 4):
        t = t + s[48 * j : 48 * j + 48] * phiy[j : j + 1]
    level = lax.broadcasted_iota(jnp.int32, (L, width), 0).astype(f32)
    hat = jnp.maximum(0.0, 1.0 - jnp.abs(z - level))
    return [jnp.sum(t[16 * c : 16 * c + 16] * hat, axis=0, keepdims=True) for c in range(3)]


def anchors(n, by):
    a = n // by
    return a.astype(f32), (n - a * by).astype(f32)


def gather_lists(pos_ref, bins_ref, list_ref, listed_ref, gone_ref, rows):
    count = bins_ref.shape[1] // LANES
    padded = rows.shape[1]
    if padded > count:
        rows[:, count:, :] = jnp.zeros((4, padded - count, LANES), f32)

    def fold(q, carry):
        at = pl.ds(pl.multiple_of(q * LANES, LANES), LANES)
        for k in range(3):
            there = pl.ds(pl.multiple_of((k * count + q) * LANES, LANES), LANES)
            rows[k, pl.ds(q, 1), :] = pos_ref[:, there]
        rows[3, pl.ds(q, 1), :] = bins_ref[:, at].astype(f32)
        return carry

    lax.fori_loop(0, count, fold, 0, unroll=8)
    slots = list_ref[...]
    hi_index = slots >> 7
    lo_index = jnp.where(slots >= 0, slots & 127, -1)
    hot_hi = hot_rows(padded, hi_index).astype(bf16)
    hot_lo = hot_rows(LANES, lo_index)
    gone_ref[...] = mm(hot_hi, hot_lo.astype(bf16), 1, 1)
    for k in range(4):
        turned = rows[k].T
        parts = thirds(turned) if k < 3 else (turned.astype(bf16),)
        y = mm(parts[0], hot_hi, 1, 0)
        for part in parts[1:]:
            y = y + mm(part, hot_hi, 1, 0)
        listed_ref[k : k + 1, :] = jnp.sum(y * hot_lo, axis=0, keepdims=True)


def grid_peers(sizes):
    regions, subs = sizes
    r, s = lax.axis_index("region"), lax.axis_index("sub")

    def present(d):
        a, b = r + compass[d][0], s + compass[d][1]
        return (a >= 0) & (a < regions) & (b >= 0) & (b < subs)

    def target(d):
        return {"region": r + compass[d][0], "sub": s + compass[d][1]}

    return present, target


def greet(present, target):
    barrier = pltpu.get_barrier_semaphore()
    peers = jnp.int32(0)
    for d in range(8):
        peers = peers + jnp.where(present(d), 1, 0)

        @pl.when(present(d))
        def _():
            pl.semaphore_signal(barrier, inc=1, device_id=target(d), device_id_type=MESH)
    pl.semaphore_wait(barrier, peers)


def coef_kernel(
    sizes, vel_far, rbf_far, pos, bins, lists, tab, pay, fin, gone,
    vel, rbf, west, east, north, south, corners, acc, tabf, listed, folded, send, recv, near,
):
    bx, by = vel.shape[0], vel.shape[1]
    blocks = bx * by
    fetches = [
        pltpu.make_async_copy(vel_far, vel, near.at[0]),
        pltpu.make_async_copy(rbf_far, rbf, near.at[1]),
    ]
    present, target = grid_peers(sizes)
    for box in (west, east, north, south, corners):
        box[...] = jnp.zeros(box.shape, f32)
    greet(present, target)
    boxes = [corners.at[0], north, corners.at[1], west, east, corners.at[2], south, corners.at[3]]

    def halo(e):
        dr, dc = compass[e]
        row_at = 0 if dr < 0 else bx - 1
        col_at = 0 if dc < 0 else by - 1
        if dr == 0:
            src = vel_far.at[:, col_at]
        elif dc == 0:
            src = vel_far.at[row_at]
        else:
            src = vel_far.at[row_at, col_at]
        return pltpu.make_async_remote_copy(
            src_ref=src, dst_ref=boxes[7 - e], send_sem=send.at[e], recv_sem=recv.at[7 - e],
            device_id=target(e), device_id_type=MESH,
        )

    for e in (3, 4, 0, 2, 5, 7, 1, 6):
        @pl.when(present(e))
        def _():
            halo(e).start()

    for fetch in fetches:
        fetch.start()
    gather_lists(pos, bins, lists, listed, gone, folded)
    acc[...] = jnp.zeros(acc.shape, f32)

    def row(source, targets, columns):
        for j in columns:
            v = source(j)
            vhi, vlo = halves(v)
            vcat = jnp.concatenate([vhi, vlo, vhi], axis=1)
            places, pieces = [], []
            for ti, u in targets:
                safe = jnp.clip(ti, 0, bx - 1)
                for tj in range(max(0, j - 1), min(by - 1, j + 1) + 1):
                    seg = 3 * (u + 1) + (j - tj + 1)
                    pieces.append(rbf[safe, tj, :, seg * 128 : (seg + 1) * 128])
                    places.append(((ti + 1) * by + tj) * NB)
            whi, wlo = halves(jnp.concatenate(pieces, axis=0))
            out = mm(jnp.concatenate([whi, whi, wlo], axis=1), vcat, 1, 1)
            for k, place in enumerate(places):
                at = pl.ds(pl.multiple_of(place, NB), NB)
                acc[at, :] += out[k * NB : (k + 1) * NB]

    def north_at(j):
        return corners[0] if j < 0 else corners[1] if j == by else north[j]

    def south_at(j):
        return corners[2] if j < 0 else corners[3] if j == by else south[j]

    def around(i):
        return [(i - 1, 1), (i, 0), (i + 1, -1)]

    def inner(i, carry):
        row(lambda j: vel[i, j], around(i), range(by))
        return carry

    def outer(i, carry):
        row(lambda j: west[i] if j < 0 else east[i], around(i), (-1, by))
        return carry

    for fetch in fetches:
        fetch.wait()
    lax.fori_loop(0, bx, inner, 0)
    for e in range(8):
        @pl.when(present(e))
        def _():
            halo(e).wait_send()
    for e in range(8):
        @pl.when(present(e))
        def _():
            halo(7 - e).wait_recv()
    row(north_at, [(jnp.int32(0), -1)], range(-1, by + 1))
    row(south_at, [(jnp.int32(bx - 1), 1)], range(-1, by + 1))
    lax.fori_loop(0, bx, outer, 0)

    for jy in range(4):
        for pair in range(2):
            both = []
            for jx in (2 * pair, 2 * pair + 1):
                both.append(acc[pl.ds(by * NB + jx * 4 + jy, blocks, stride=NB), :])
            t = jnp.concatenate(both, axis=0).T
            columns = slice(pair * 2 * blocks, (pair + 1) * 2 * blocks)
            tabf[0, jy * 48 : jy * 48 + 48, columns] = t[0:48]
            tabf[1, jy * 48 : jy * 48 + 48, columns] = 0.5 * (t[0:48] + t[48:96])
    for m in range(2):
        hi, lo = halves(tabf[m])
        tab[m] = jnp.concatenate([hi, lo, hi], axis=1)

    per = CHUNK // MIG
    for c in range(lists.shape[1] // CHUNK):
        at = slice(c * CHUNK, (c + 1) * CHUNK)
        x, y, z = listed[0:1, at], listed[1:2, at], listed[2:3, at]
        n = (listed[3:4, at] + 0.5).astype(jnp.int32)
        flags = jnp.where(lists[:, at] >= 0, 1.0, 0.0)
        ax, ay = anchors(n, by)
        hot = hot_rows(blocks, n).astype(bf16)
        u = velocity_at(x, y, z, ax, ay, hot, tab[0])
        mx, my, mz = [p + 0.5 * time_step * q for p, q in zip((x, y, z), u)]
        first = c * per
        if first < 8:
            for k in range(per):
                d = first + k
                dr, dc = compass[d]
                sl = slice(k * MIG, (k + 1) * MIG)
                fl = flags[:, sl]
                na = jnp.clip(ax[:, sl] - float(dr * bx), 0.0, float(bx - 1))
                nb = jnp.clip(ay[:, sl] - float(dc * by), 0.0, float(by - 1))
                values = [
                    x[:, sl] - float(dr * bx), y[:, sl] - float(dc * by), z[:, sl],
                    mx[:, sl] - float(dr * bx), my[:, sl] - float(dc * by), mz[:, sl],
                    na * float(by) + nb,
                ]
                for r, v in enumerate(values):
                    pay[d, r : r + 1, :] = v * fl
                pay[d, 7:8, :] = fl
        else:
            u = velocity_at(mx, my, mz, ax, ay, hot, tab[1])
            there = slice((first - 8) * MIG, (first - 8 + per) * MIG)
            for k, (p, q) in enumerate(zip((x, y, z), u)):
                fin[k : k + 1, there] = p + time_step * q


def step_kernel(
    sizes, shape, split, live, pos, bins, gone, tab, pay, fin, leaving,
    out, land, box0, box1, pay1, spread, send0, recv0, send1, recv1,
):
    bx, by = shape
    blocks = bx * by
    present, target = grid_peers(sizes)
    box0[...] = jnp.zeros(box0.shape, f32)
    box1[...] = jnp.zeros(box1.shape, f32)
    greet(present, target)

    def parcel(d, src, box, send, recv):
        return pltpu.make_async_remote_copy(
            src_ref=src.at[d], dst_ref=box.at[7 - d], send_sem=send.at[d],
            recv_sem=recv.at[7 - d], device_id=target(d), device_id_type=MESH,
        )

    def post(src, box, send, recv):
        for d in range(8):
            @pl.when(present(d))
            def _():
                parcel(d, src, box, send, recv).start()

    def collect(src, box, send, recv):
        for d in range(8):
            @pl.when(present(d))
            def _():
                parcel(d, src, box, send, recv).wait_send()
        for d in range(8):
            @pl.when(present(d))
            def _():
                parcel(7 - d, src, box, send, recv).wait_recv()

    resident = live[0, 0]
    cap = bins.shape[1]
    arrivals = 8 * MIG
    most = cap - 2 * arrivals
    width = most // PARTS
    for k in range(3):
        out[:, k * cap + most : (k + 1) * cap] = jnp.zeros((1, cap - most), f32)

    def bulk(i, carry):
        at = pl.ds(pl.multiple_of(i * width, LANES), width)
        slot = lax.broadcasted_iota(jnp.int32, (1, width), 1) + i * width
        alive = slot < resident
        ats = [pl.ds(pl.multiple_of(k * cap + i * width, LANES), width) for k in range(3)]
        x, y, z = [jnp.where(alive, pos[:, there], 0.0) for there in ats]
        n = bins[:, at]
        left = jnp.concatenate(
            [gone[pl.ds(i * (width // LANES) + k, 1), :] for k in range(width // LANES)], axis=1
        )
        ax, ay = anchors(n, by)
        hot = hot_rows(blocks, n).astype(bf16)
        u = velocity_at(x, y, z, ax, ay, hot, tab[0])
        mx, my, mz = [p + 0.5 * time_step * q for p, q in zip((x, y, z), u)]
        u = velocity_at(mx, my, mz, ax, ay, hot, tab[1])
        keep = alive & (left == 0.0)
        for k, (p, q) in enumerate(zip((x, y, z), u)):
            out[:, ats[k]] = jnp.where(keep, p + time_step * q, 0.0)
        return carry

    post(pay, box0, send0, recv0)
    lax.fori_loop(0, split, bulk, 0)
    collect(pay, box0, send0, recv0)

    per = CHUNK // MIG
    living = []
    for c in range(8 // per):
        rows = [
            jnp.concatenate([box0[c * per + k, q : q + 1, :] for k in range(per)], axis=1)
            for q in range(8)
        ]
        n = (rows[6] + 0.5).astype(jnp.int32)
        ax, ay = anchors(n, by)
        hot = hot_rows(blocks, n).astype(bf16)
        u = velocity_at(rows[3], rows[4], rows[5], ax, ay, hot, tab[1])
        living.append(rows[7])
        for k in range(3):
            f = rows[k] + time_step * u[k]
            begin = 2 * k * arrivals + c * CHUNK
            land[:, begin : begin + CHUNK] = f
            for e in range(per):
                spread[c * per + e : c * per + e + 1, k * LANES : (k + 1) * LANES] = f[
                    :, e * LANES : (e + 1) * LANES
                ]

    slots = leaving[...]
    flags = jnp.where(slots >= 0, 1.0, 0.0)
    late = slots >= resident
    rel = jnp.where(late & (slots >= 0), slots - resident, -1)
    hot_hi = hot_rows(8, rel >> 7)
    hot_lo = hot_rows(LANES, jnp.where(rel >= 0, rel & 127, -1))
    hot_bf = jnp.concatenate([hot_hi, jnp.zeros(hot_hi.shape, f32)], axis=0).astype(bf16)
    left = mm(hot_bf, hot_lo.astype(bf16), 1, 1)
    wide = spread[...]
    wide = jnp.concatenate([wide, jnp.zeros(wide.shape, f32)], axis=0)
    picked = None
    for part in thirds(wide):
        y = mm(part, hot_bf, 0, 0)
        picked = y if picked is None else picked + y
    for k in range(3):
        mine = jnp.sum(picked[k * LANES : (k + 1) * LANES] * hot_lo, axis=0, keepdims=True)
        value = jnp.where(late, mine, fin[k : k + 1, :])
        for d in range(8):
            sl = slice(d * MIG, (d + 1) * MIG)
            shift = float((bx * compass[d][0], by * compass[d][1], 0)[k])
            pay1[d, k : k + 1, :] = (value[:, sl] - shift) * flags[:, sl]
    for d in range(8):
        pay1[d, 3:4, :] = flags[:, d * MIG : (d + 1) * MIG]
        pay1[d, 4:8, :] = jnp.zeros((4, MIG), f32)

    post(pay1, box1, send1, recv1)
    for d in range(8):
        sl = slice(d * MIG, (d + 1) * MIG)
        stays = jnp.where(left[d : d + 1] == 0.0, 1.0, 0.0)
        stays = stays * living[d // per][:, (d % per) * MIG : (d % per + 1) * MIG]
        for k in range(3):
            begin = 2 * k * arrivals + d * MIG
            land[:, begin : begin + MIG] = land[:, begin : begin + MIG] * stays
    lax.fori_loop(split, PARTS, bulk, 0)
    collect(pay1, box1, send1, recv1)
    for d in range(8):
        for k in range(3):
            begin = (2 * k + 1) * arrivals + d * MIG
            land[:, begin : begin + MIG] = box1[d, k : k + 1, :] * box1[d, 3:4, :]


def body(sizes, velocity, rbf_coef, positions, cell_bins, live_count, departures):
    bx, by, _, c3l, cb = velocity.shape
    cap = positions.shape[-1]
    count = 8 * MIG
    vel = velocity.reshape(bx, by, 2 * c3l, cb)
    rbf = rbf_coef
    pos = positions.reshape(1, 3 * cap)
    bins = cell_bins.reshape(1, cap)
    lists = departures.reshape(1, 2 * count)
    vmem = pl.BlockSpec(memory_space=pltpu.VMEM)
    smem = pl.BlockSpec(memory_space=pltpu.SMEM)
    rows = -(-(cap // LANES) // 128) * 128
    blocks = bx * by
    tab, pay, fin, gone = pl.pallas_call(
        functools.partial(coef_kernel, sizes),
        out_shape=(
            jax.ShapeDtypeStruct((2, 192, 12 * blocks), bf16),
            jax.ShapeDtypeStruct((8, 8, MIG), f32),
            jax.ShapeDtypeStruct((3, count), f32),
            jax.ShapeDtypeStruct((rows, LANES), f32),
        ),
        in_specs=[pl.BlockSpec(memory_space=pl.ANY)] * 2 + [vmem] * 3,
        out_specs=(vmem,) * 4,
        scratch_shapes=[
            pltpu.VMEM(vel.shape, f32),
            pltpu.VMEM(rbf.shape, f32),
            pltpu.VMEM((bx, 2 * c3l, cb), f32),
            pltpu.VMEM((bx, 2 * c3l, cb), f32),
            pltpu.VMEM((by, 2 * c3l, cb), f32),
            pltpu.VMEM((by, 2 * c3l, cb), f32),
            pltpu.VMEM((4, 2 * c3l, cb), f32),
            pltpu.VMEM(((bx + 2) * by * NB, 2 * c3l), f32),
            pltpu.VMEM((2, 192, 4 * blocks), f32),
            pltpu.VMEM((4, 2 * count), f32),
            pltpu.VMEM((4, rows, LANES), f32),
            pltpu.SemaphoreType.DMA((8,)),
            pltpu.SemaphoreType.DMA((8,)),
            pltpu.SemaphoreType.DMA((2,)),
        ],
        compiler_params=pltpu.CompilerParams(
            collective_id=1, has_side_effects=True, vmem_limit_bytes=VMEM_LIMIT
        ),
        name="coefficients",
    )(vel, rbf, pos, bins, lists)

    out, land = pl.pallas_call(
        functools.partial(step_kernel, sizes, (bx, by), 2),
        out_shape=(
            jax.ShapeDtypeStruct((1, 3 * cap), f32),
            jax.ShapeDtypeStruct((1, 6 * count), f32),
        ),
        in_specs=[smem] + [vmem] * 7,
        out_specs=(vmem,) * 2,
        scratch_shapes=[
            pltpu.VMEM((8, 8, MIG), f32),
            pltpu.VMEM((8, 8, MIG), f32),
            pltpu.VMEM((8, 8, MIG), f32),
            pltpu.VMEM((8, 3 * LANES), f32),
            pltpu.SemaphoreType.DMA((8,)),
            pltpu.SemaphoreType.DMA((8,)),
            pltpu.SemaphoreType.DMA((8,)),
            pltpu.SemaphoreType.DMA((8,)),
        ],
        compiler_params=pltpu.CompilerParams(
            collective_id=0, has_side_effects=True, vmem_limit_bytes=VMEM_LIMIT
        ),
        name="advect",
    )(live_count, pos, bins, gone, tab, pay, fin, lists[:, count:])
    resident = live_count[0, 0]
    for k in range(3):
        piece = land[:, 2 * count * k : 2 * count * (k + 1)]
        out = lax.dynamic_update_slice(out, piece, (jnp.int32(0), k * cap + resident))
    return out.reshape(1, 1, 3, cap)


def solution(mesh):
    in_specs = (
        P(("member", "region"), "sub", None, None, None),
        P("region", "sub", None, None),
        P(("member", "region"), "sub", None, None),
        P(("member", "region"), "sub", None),
        P(("member", "region"), "sub"),
        P(("member", "region"), "sub", None, None, None),
    )
    out_specs = P(("member", "region"), "sub", None, None)
    sizes = (mesh.shape["region"], mesh.shape["sub"])
    return jax.shard_map(
        functools.partial(body, sizes), mesh=mesh, in_specs=in_specs, out_specs=out_specs,
        check_vma=False,
    )
```

```python
import functools
import jax
import jax.numpy as jnp
from jax import lax
from jax.experimental import pallas as pl
from jax.experimental.pallas import tpu as pltpu
from jax.sharding import PartitionSpec as P

L = 16
NB = 16
MIG = 128
LANES = 128
CHUNK = 1024
PARTS = 8

time_step = 0.1
compass = ((-1, -1), (-1, 0), (-1, 1), (0, -1), (0, 1), (1, -1), (1, 0), (1, 1))

MESH = pl.DeviceIdType.MESH
f32 = jnp.float32
bf16 = jnp.bfloat16
VMEM_LIMIT = 56 * 2**20


def halves(v):
    hi = v.astype(bf16)
    return hi, (v - hi.astype(f32)).astype(bf16)


def thirds(v):
    hi = v.astype(bf16)
    rest = v - hi.astype(f32)
    mid = rest.astype(bf16)
    return hi, mid, (rest - mid.astype(f32)).astype(bf16)


def mm(a, b, ca, cb):
    return lax.dot_general(a, b, (((ca,), (cb,)), ((), ())), preferred_element_type=f32)


def hot_rows(rows, which):
    ids = lax.broadcasted_iota(jnp.int32, (rows, which.shape[1]), 0)
    return jnp.where(ids == which, 1.0, 0.0)


def velocity_at(x, y, z, ax, ay, hot, table):
    width = x.shape[1]
    centre = (lax.broadcasted_iota(jnp.int32, (4, width), 0).astype(f32) + 0.5) * 0.25
    dx = (x - ax) - centre
    dy = (y - ay) - centre
    phix = jnp.exp(dx * dx * (-1.0 / 0.18))
    phiy = jnp.exp(dy * dy * (-1.0 / 0.18))
    hi, lo = halves(phix)
    hi, lo = hi.astype(f32), lo.astype(f32)
    high, low = [], []
    for j in range(4):
        high.append(hot * jnp.broadcast_to(hi[j : j + 1], hot.shape).astype(bf16))
        low.append(hot * jnp.broadcast_to(lo[j : j + 1], hot.shape).astype(bf16))
    feats = jnp.concatenate(high + high + low, axis=0)
    s = mm(table, feats, 1, 0)
    t = s[0:48] * phiy[0:1]
    for j in range(1, 4):
        t = t + s[48 * j : 48 * j + 48] * phiy[j : j + 1]
    level = lax.broadcasted_iota(jnp.int32, (L, width), 0).astype(f32)
    hat = jnp.maximum(0.0, 1.0 - jnp.abs(z - level))
    return [jnp.sum(t[16 * c : 16 * c + 16] * hat, axis=0, keepdims=True) for c in range(3)]


def anchors(n, by):
    a = n // by
    return a.astype(f32), (n - a * by).astype(f32)


def gather_lists(pos_ref, bins_ref, list_ref, listed_ref, gone_ref, rows):
    count = bins_ref.shape[1] // LANES
    padded = rows.shape[1]
    if padded > count:
        rows[:, count:, :] = jnp.zeros((4, padded - count, LANES), f32)

    def fold(q, carry):
        at = pl.ds(pl.multiple_of(q * LANES, LANES), LANES)
        for k in range(3):
            there = pl.ds(pl.multiple_of((k * count + q) * LANES, LANES), LANES)
            rows[k, pl.ds(q, 1), :] = pos_ref[:, there]
        rows[3, pl.ds(q, 1), :] = bins_ref[:, at].astype(f32)
        return carry

    lax.fori_loop(0, count, fold, 0, unroll=8)
    slots = list_ref[...]
    hi_index = slots >> 7
    lo_index = jnp.where(slots >= 0, slots & 127, -1)
    hot_hi = hot_rows(padded, hi_index).astype(bf16)
    hot_lo = hot_rows(LANES, lo_index)
    gone_ref[...] = mm(hot_hi, hot_lo.astype(bf16), 1, 1)
    for k in range(4):
        turned = rows[k].T
        parts = thirds(turned) if k < 3 else (turned.astype(bf16),)
        y = mm(parts[0], hot_hi, 1, 0)
        for part in parts[1:]:
            y = y + mm(part, hot_hi, 1, 0)
        listed_ref[k : k + 1, :] = jnp.sum(y * hot_lo, axis=0, keepdims=True)


def grid_peers(sizes):
    regions, subs = sizes
    r, s = lax.axis_index("region"), lax.axis_index("sub")

    def present(d):
        a, b = r + compass[d][0], s + compass[d][1]
        return (a >= 0) & (a < regions) & (b >= 0) & (b < subs)

    def target(d):
        return {"region": r + compass[d][0], "sub": s + compass[d][1]}

    return present, target


def greet(present, target):
    barrier = pltpu.get_barrier_semaphore()
    peers = jnp.int32(0)
    for d in range(8):
        peers = peers + jnp.where(present(d), 1, 0)

        @pl.when(present(d))
        def _():
            pl.semaphore_signal(barrier, inc=1, device_id=target(d), device_id_type=MESH)
    pl.semaphore_wait(barrier, peers)


def coef_kernel(
    sizes, vel_far, rbf_far, pos, bins, lists, tab, pay, fin, gone,
    vel, rbf, west, east, north, south, corners, acc, tabf, listed, folded, send, recv, near,
):
    bx, by = vel.shape[0], vel.shape[1]
    blocks = bx * by
    fetches = [
        pltpu.make_async_copy(vel_far, vel, near.at[0]),
        pltpu.make_async_copy(rbf_far, rbf, near.at[1]),
    ]
    present, target = grid_peers(sizes)
    for box in (west, east, north, south, corners):
        box[...] = jnp.zeros(box.shape, f32)
    greet(present, target)
    boxes = [corners.at[0], north, corners.at[1], west, east, corners.at[2], south, corners.at[3]]

    def halo(e):
        dr, dc = compass[e]
        row_at = 0 if dr < 0 else bx - 1
        col_at = 0 if dc < 0 else by - 1
        if dr == 0:
            src = vel_far.at[:, col_at]
        elif dc == 0:
            src = vel_far.at[row_at]
        else:
            src = vel_far.at[row_at, col_at]
        return pltpu.make_async_remote_copy(
            src_ref=src, dst_ref=boxes[7 - e], send_sem=send.at[e], recv_sem=recv.at[7 - e],
            device_id=target(e), device_id_type=MESH,
        )

    for e in (3, 4, 0, 2, 5, 7, 1, 6):
        @pl.when(present(e))
        def _():
            halo(e).start()

    for fetch in fetches:
        fetch.start()
    gather_lists(pos, bins, lists, listed, gone, folded)
    acc[...] = jnp.zeros(acc.shape, f32)

    def row(source, targets, columns):
        for j in columns:
            v = source(j)
            vhi, vlo = halves(v)
            vcat = jnp.concatenate([vhi, vlo, vhi], axis=1)
            places, pieces = [], []
            for ti, u in targets:
                safe = jnp.clip(ti, 0, bx - 1)
                for tj in range(max(0, j - 1), min(by - 1, j + 1) + 1):
                    seg = 3 * (u + 1) + (j - tj + 1)
                    pieces.append(rbf[safe, tj, :, seg * 128 : (seg + 1) * 128])
                    places.append(((ti + 1) * by + tj) * NB)
            whi, wlo = halves(jnp.concatenate(pieces, axis=0))
            out = mm(jnp.concatenate([whi, whi, wlo], axis=1), vcat, 1, 1)
            for k, place in enumerate(places):
                at = pl.ds(pl.multiple_of(place, NB), NB)
                acc[at, :] += out[k * NB : (k + 1) * NB]

    def north_at(j):
        return corners[0] if j < 0 else corners[1] if j == by else north[j]

    def south_at(j):
        return corners[2] if j < 0 else corners[3] if j == by else south[j]

    def around(i):
        return [(i - 1, 1), (i, 0), (i + 1, -1)]

    def inner(i, carry):
        row(lambda j: vel[i, j], around(i), range(by))
        return carry

    def outer(i, carry):
        row(lambda j: west[i] if j < 0 else east[i], around(i), (-1, by))
        return carry

    for fetch in fetches:
        fetch.wait()
    lax.fori_loop(0, bx, inner, 0)
    for e in range(8):
        @pl.when(present(e))
        def _():
            halo(e).wait_send()
    for e in range(8):
        @pl.when(present(e))
        def _():
            halo(7 - e).wait_recv()
    row(north_at, [(jnp.int32(0), -1)], range(-1, by + 1))
    row(south_at, [(jnp.int32(bx - 1), 1)], range(-1, by + 1))
    lax.fori_loop(0, bx, outer, 0)

    for jy in range(4):
        for pair in range(2):
            both = []
            for jx in (2 * pair, 2 * pair + 1):
                both.append(acc[pl.ds(by * NB + jx * 4 + jy, blocks, stride=NB), :])
            t = jnp.concatenate(both, axis=0).T
            columns = slice(pair * 2 * blocks, (pair + 1) * 2 * blocks)
            tabf[0, jy * 48 : jy * 48 + 48, columns] = t[0:48]
            tabf[1, jy * 48 : jy * 48 + 48, columns] = 0.5 * (t[0:48] + t[48:96])
    for m in range(2):
        hi, lo = halves(tabf[m])
        tab[m] = jnp.concatenate([hi, lo, hi], axis=1)

    per = CHUNK // MIG
    for c in range(lists.shape[1] // CHUNK):
        at = slice(c * CHUNK, (c + 1) * CHUNK)
        x, y, z = listed[0:1, at], listed[1:2, at], listed[2:3, at]
        n = (listed[3:4, at] + 0.5).astype(jnp.int32)
        flags = jnp.where(lists[:, at] >= 0, 1.0, 0.0)
        ax, ay = anchors(n, by)
        hot = hot_rows(blocks, n).astype(bf16)
        u = velocity_at(x, y, z, ax, ay, hot, tab[0])
        mx, my, mz = [p + 0.5 * time_step * q for p, q in zip((x, y, z), u)]
        first = c * per
        if first < 8:
            for k in range(per):
                d = first + k
                dr, dc = compass[d]
                sl = slice(k * MIG, (k + 1) * MIG)
                fl = flags[:, sl]
                na = jnp.clip(ax[:, sl] - float(dr * bx), 0.0, float(bx - 1))
                nb = jnp.clip(ay[:, sl] - float(dc * by), 0.0, float(by - 1))
                values = [
                    x[:, sl] - float(dr * bx), y[:, sl] - float(dc * by), z[:, sl],
                    mx[:, sl] - float(dr * bx), my[:, sl] - float(dc * by), mz[:, sl],
                    na * float(by) + nb,
                ]
                for r, v in enumerate(values):
                    pay[d, r : r + 1, :] = v * fl
                pay[d, 7:8, :] = fl
        else:
            u = velocity_at(mx, my, mz, ax, ay, hot, tab[1])
            there = slice((first - 8) * MIG, (first - 8 + per) * MIG)
            for k, (p, q) in enumerate(zip((x, y, z), u)):
                fin[k : k + 1, there] = p + time_step * q


def step_kernel(
    sizes, shape, split, live, pos, bins, gone, tab, pay, fin, leaving,
    out, land, box0, box1, pay1, spread, send0, recv0, send1, recv1,
):
    bx, by = shape
    blocks = bx * by
    present, target = grid_peers(sizes)
    box0[...] = jnp.zeros(box0.shape, f32)
    box1[...] = jnp.zeros(box1.shape, f32)
    greet(present, target)

    def parcel(d, src, box, send, recv):
        return pltpu.make_async_remote_copy(
            src_ref=src.at[d], dst_ref=box.at[7 - d], send_sem=send.at[d],
            recv_sem=recv.at[7 - d], device_id=target(d), device_id_type=MESH,
        )

    def post(src, box, send, recv):
        for d in range(8):
            @pl.when(present(d))
            def _():
                parcel(d, src, box, send, recv).start()

    def collect(src, box, send, recv):
        for d in range(8):
            @pl.when(present(d))
            def _():
                parcel(d, src, box, send, recv).wait_send()
        for d in range(8):
            @pl.when(present(d))
            def _():
                parcel(7 - d, src, box, send, recv).wait_recv()

    resident = live[0, 0]
    cap = bins.shape[1]
    arrivals = 8 * MIG
    most = cap - 2 * arrivals
    width = most // PARTS
    out[:, most:] = jnp.zeros((3, cap - most), f32)

    def bulk(i, carry):
        at = pl.ds(pl.multiple_of(i * width, LANES), width)
        slot = lax.broadcasted_iota(jnp.int32, (1, width), 1) + i * width
        alive = slot < resident
        ats = [pl.ds(pl.multiple_of(k * cap + i * width, LANES), width) for k in range(3)]
        x, y, z = [jnp.where(alive, pos[:, there], 0.0) for there in ats]
        n = bins[:, at]
        left = jnp.concatenate(
            [gone[pl.ds(i * (width // LANES) + k, 1), :] for k in range(width // LANES)], axis=1
        )
        ax, ay = anchors(n, by)
        hot = hot_rows(blocks, n).astype(bf16)
        u = velocity_at(x, y, z, ax, ay, hot, tab[0])
        mx, my, mz = [p + 0.5 * time_step * q for p, q in zip((x, y, z), u)]
        u = velocity_at(mx, my, mz, ax, ay, hot, tab[1])
        keep = alive & (left == 0.0)
        for k, (p, q) in enumerate(zip((x, y, z), u)):
            out[k : k + 1, at] = jnp.where(keep, p + time_step * q, 0.0)
        return carry

    post(pay, box0, send0, recv0)
    lax.fori_loop(0, split, bulk, 0)
    collect(pay, box0, send0, recv0)

    per = CHUNK // MIG
    living = []
    for c in range(8 // per):
        rows = [
            jnp.concatenate([box0[c * per + k, q : q + 1, :] for k in range(per)], axis=1)
            for q in range(8)
        ]
        n = (rows[6] + 0.5).astype(jnp.int32)
        ax, ay = anchors(n, by)
        hot = hot_rows(blocks, n).astype(bf16)
        u = velocity_at(rows[3], rows[4], rows[5], ax, ay, hot, tab[1])
        living.append(rows[7])
        for k in range(3):
            f = rows[k] + time_step * u[k]
            land[k : k + 1, c * CHUNK : (c + 1) * CHUNK] = f
            for e in range(per):
                spread[c * per + e : c * per + e + 1, k * LANES : (k + 1) * LANES] = f[
                    :, e * LANES : (e + 1) * LANES
                ]

    slots = leaving[:, arrivals:]
    flags = jnp.where(slots >= 0, 1.0, 0.0)
    late = slots >= resident
    rel = jnp.where(late & (slots >= 0), slots - resident, -1)
    hot_hi = hot_rows(8, rel >> 7)
    hot_lo = hot_rows(LANES, jnp.where(rel >= 0, rel & 127, -1))
    hot_bf = jnp.concatenate([hot_hi, jnp.zeros(hot_hi.shape, f32)], axis=0).astype(bf16)
    left = mm(hot_bf, hot_lo.astype(bf16), 1, 1)
    wide = spread[...]
    wide = jnp.concatenate([wide, jnp.zeros(wide.shape, f32)], axis=0)
    picked = None
    for part in thirds(wide):
        y = mm(part, hot_bf, 0, 0)
        picked = y if picked is None else picked + y
    for k in range(3):
        mine = jnp.sum(picked[k * LANES : (k + 1) * LANES] * hot_lo, axis=0, keepdims=True)
        value = jnp.where(late, mine, fin[k : k + 1, :])
        for d in range(8):
            sl = slice(d * MIG, (d + 1) * MIG)
            shift = float((bx * compass[d][0], by * compass[d][1], 0)[k])
            pay1[d, k : k + 1, :] = (value[:, sl] - shift) * flags[:, sl]
    for d in range(8):
        pay1[d, 3:4, :] = flags[:, d * MIG : (d + 1) * MIG]
        pay1[d, 4:8, :] = jnp.zeros((4, MIG), f32)

    post(pay1, box1, send1, recv1)
    for d in range(8):
        sl = slice(d * MIG, (d + 1) * MIG)
        stays = jnp.where(left[d : d + 1] == 0.0, 1.0, 0.0)
        stays = stays * living[d // per][:, (d % per) * MIG : (d % per + 1) * MIG]
        land[:, sl] = land[:, sl] * stays
    lax.fori_loop(split, PARTS, bulk, 0)
    collect(pay1, box1, send1, recv1)
    for d in range(8):
        for k in range(3):
            begin = arrivals + d * MIG
            land[k : k + 1, begin : begin + MIG] = box1[d, k : k + 1, :] * box1[d, 3:4, :]


def body(sizes, velocity, rbf_coef, positions, cell_bins, live_count, departures):
    bx, by, _, c3l, cb = velocity.shape
    cap = positions.shape[-1]
    count = 8 * MIG
    vel = velocity.reshape(bx, by, 2 * c3l, cb)
    rbf = rbf_coef
    pos = positions.reshape(1, 3 * cap)
    bins = cell_bins.reshape(1, cap)
    lists = departures.reshape(1, 2 * count)
    vmem = pl.BlockSpec(memory_space=pltpu.VMEM)
    smem = pl.BlockSpec(memory_space=pltpu.SMEM)
    rows = -(-(cap // LANES) // 128) * 128
    blocks = bx * by
    tab, pay, fin, gone = pl.pallas_call(
        functools.partial(coef_kernel, sizes),
        out_shape=(
            jax.ShapeDtypeStruct((2, 192, 12 * blocks), bf16),
            jax.ShapeDtypeStruct((8, 8, MIG), f32),
            jax.ShapeDtypeStruct((3, count), f32),
            jax.ShapeDtypeStruct((rows, LANES), f32),
        ),
        in_specs=[pl.BlockSpec(memory_space=pl.ANY)] * 2 + [vmem] * 3,
        out_specs=(vmem,) * 4,
        scratch_shapes=[
            pltpu.VMEM(vel.shape, f32),
            pltpu.VMEM(rbf.shape, f32),
            pltpu.VMEM((bx, 2 * c3l, cb), f32),
            pltpu.VMEM((bx, 2 * c3l, cb), f32),
            pltpu.VMEM((by, 2 * c3l, cb), f32),
            pltpu.VMEM((by, 2 * c3l, cb), f32),
            pltpu.VMEM((4, 2 * c3l, cb), f32),
            pltpu.VMEM(((bx + 2) * by * NB, 2 * c3l), f32),
            pltpu.VMEM((2, 192, 4 * blocks), f32),
            pltpu.VMEM((4, 2 * count), f32),
            pltpu.VMEM((4, rows, LANES), f32),
            pltpu.SemaphoreType.DMA((8,)),
            pltpu.SemaphoreType.DMA((8,)),
            pltpu.SemaphoreType.DMA((2,)),
        ],
        compiler_params=pltpu.CompilerParams(
            collective_id=1, has_side_effects=True, vmem_limit_bytes=VMEM_LIMIT
        ),
        name="coefficients",
    )(vel, rbf, pos, bins, lists)

    out, land = pl.pallas_call(
        functools.partial(step_kernel, sizes, (bx, by), 2),
        out_shape=(
            jax.ShapeDtypeStruct((3, cap), f32),
            jax.ShapeDtypeStruct((3, 2 * count), f32),
        ),
        in_specs=[smem] + [vmem] * 7,
        out_specs=(vmem,) * 2,
        scratch_shapes=[
            pltpu.VMEM((8, 8, MIG), f32),
            pltpu.VMEM((8, 8, MIG), f32),
            pltpu.VMEM((8, 8, MIG), f32),
            pltpu.VMEM((8, 3 * LANES), f32),
            pltpu.SemaphoreType.DMA((8,)),
            pltpu.SemaphoreType.DMA((8,)),
            pltpu.SemaphoreType.DMA((8,)),
            pltpu.SemaphoreType.DMA((8,)),
        ],
        compiler_params=pltpu.CompilerParams(
            collective_id=0, has_side_effects=True, vmem_limit_bytes=VMEM_LIMIT
        ),
        name="advect",
    )(live_count, pos, bins, gone, tab, pay, fin, lists)
    resident = live_count[0, 0]
    return lax.dynamic_update_slice(out, land, (jnp.int32(0), resident))[None, None]


def solution(mesh):
    in_specs = (
        P(("member", "region"), "sub", None, None, None),
        P("region", "sub", None, None),
        P(("member", "region"), "sub", None, None),
        P(("member", "region"), "sub", None),
        P(("member", "region"), "sub"),
        P(("member", "region"), "sub", None, None, None),
    )
    out_specs = P(("member", "region"), "sub", None, None)
    sizes = (mesh.shape["region"], mesh.shape["sub"])
    return jax.shard_map(
        functools.partial(body, sizes), mesh=mesh, in_specs=in_specs, out_specs=out_specs,
        check_vma=False,
    )
```
